32 devices in a mesh: wide: 16 (over z, y, x), narrow: 2 (over core).
Axes of the slice: x: 2, y: 2, z: 4, core: 2. Of those that a mesh axis runs over, the one named last changes fastest.
Arguments:
- effects_start: float32 [16384, 256], P(('wide', 'narrow')), may hold values from -3 to 3
- marginal: float32 [16384, 256], P(('wide', 'narrow')), may hold values from -6 to 6
- ld_diag: float32 [16384, 512], P(('wide', 'narrow')), may hold values from -1 to 1, as said below
- ld_upper: float32 [16384, 512], P(('wide', 'narrow')), may hold values from -1 to 1
- penalty_grid: float32 [16], replicated, may hold values from 0.1 to 1
- penalty_index: int32 [256], replicated, may hold values from 0 to 15
- dosages: bfloat16 [64, 16384], P(None, ('wide', 'narrow')), may hold values from 0 to 2
- stack_weights: float32 [256, 256], replicated, may hold values from -0.375 to 0.375
Outputs:
- effects: float32 [16384, 256], P(('wide', 'narrow'))
- stacked: float32 [64, 256], P(('wide', 'narrow'))
The draws below stay inside these ranges and needn't reach their ends.
Inputs may be any that keep to these rules, and one draw needn't show every extreme that they name: `ld_diag`: each diagonal tile is symmetric.
All inputs are finite; a program needn't handle non-finite values.
Results may differ from the reference program's by a relative error of at most 0.0037.
Values sent between devices are 32-bit elements; how exact they have to be, the bound alone decides.
A program may use at most 64 MiB of HBM per device.

```python
import math
import jax
import jax.numpy as jnp
from jax import lax

VAR_DEV = 512
K = 256
LEVELS = 16
ITERS = 3
M = 16384
N_IND = 64


def tile_entries(key):
    strips = M // VAR_DEV
    raw = jnp.clip(jax.random.normal(key, (strips, VAR_DEV, VAR_DEV), jnp.float32), -4.0, 4.0)
    return raw * (0.25 / math.sqrt(VAR_DEV))


def draw_ld_diag(key, part):
    raw = tile_entries(jax.random.fold_in(key, 11))
    symmetric = (raw + jnp.swapaxes(raw, 1, 2)) / math.sqrt(2.0)
    identity = jnp.eye(VAR_DEV, dtype=jnp.float32)
    tiles = symmetric * (1.0 - identity)[None] + identity[None]
    return tiles.reshape(M, VAR_DEV)


def draw_ld_upper(key, part):
    raw = tile_entries(jax.random.fold_in(key, 23))
    return raw.reshape(M, VAR_DEV)


def with_ends(array, stream_key, least, high):
    shape = array.shape
    index_at = [jax.random.randint(jax.random.fold_in(stream_key, axis), (), 0, shape[axis]) for axis in range(len(shape))]
    array = array.at[tuple(index_at)].set(least)
    longest = shape.index(max(shape))
    index_at[longest] = (index_at[longest] + 1) % shape[longest]
    return array.at[tuple(index_at)].set(high)


def level_of(own_key, dims, pieces, low, largest):
    loudness = 1.0
    for axis_at, parts in pieces:
        heights = jax.random.uniform(jax.random.fold_in(jax.random.fold_in(own_key, 6), axis_at), (parts,), jnp.float32, low / len(pieces), largest / len(pieces))
        loudness = loudness * jnp.repeat(jnp.exp(heights), dims[axis_at] // parts).reshape((-1,) + (1,) * (len(dims) - 1 - axis_at))
    return loudness


def centred(stream_key, dims, spread, bound, shards=(), held_as=jnp.bfloat16):
    drawn = jax.random.normal(stream_key, dims, jnp.float32) * spread
    if len(shards) > 0:
        drawn = level_of(stream_key, dims, shards, -0.22, 0.18) * drawn
    return jnp.clip(drawn, min=-bound, max=bound).astype(held_as)


def setup_inputs(seed: int = 0) -> dict:
    seeds = jax.random.split(jax.random.key(seed), 9)
    effects_start = centred(seeds[0], (M, K), 0.5, 3.0, ((0, 32),), jnp.float32)
    marginal = centred(seeds[1], (M, K), 1.0, 6.0, ((0, 32),), jnp.float32)
    ld_diag = draw_ld_diag(jax.random.fold_in(seeds[8], 71), 0)
    ld_upper = draw_ld_upper(jax.random.fold_in(seeds[8], 71), 0)
    penalty_grid = jnp.clip(jnp.exp(jax.random.uniform(seeds[4], (LEVELS,), jnp.float32, math.log(0.1), math.log(1.0))), 0.1, 1.0)
    penalty_index = with_ends(jax.random.randint(seeds[5], (K,), 0, LEVELS), jax.random.fold_in(seeds[5], 1), 0, LEVELS - 1).astype(jnp.int32)
    dosages = jnp.clip(2.0 * jax.random.uniform(seeds[6], (N_IND, M), jnp.float32) ** level_of(seeds[6], (N_IND, M), ((1, 32),), -0.2, 0.2), 0.0, 2.0).astype(jnp.bfloat16)
    stack_weights = centred(seeds[7], (K, K), K ** -0.5, 0.375, (), jnp.float32)
    return dict(effects_start=effects_start, marginal=marginal, ld_diag=ld_diag, ld_upper=ld_upper, penalty_grid=penalty_grid, penalty_index=penalty_index, dosages=dosages, stack_weights=stack_weights)


step_size = 0.5

def reference(effects_start, marginal, ld_diag, ld_upper, penalty_grid, penalty_index, dosages, stack_weights):
    strips = M // VAR_DEV
    diag_blocks = ld_diag.reshape(strips, VAR_DEV, VAR_DEV)
    upper_blocks = ld_upper.reshape(strips, VAR_DEV, VAR_DEV)
    threshold = step_size * penalty_grid[penalty_index]
    effects = effects_start
    for sweep in range(ITERS):
        blocked = effects.reshape(strips, VAR_DEV, K)
        product = jnp.einsum('sij,sjk->sik', diag_blocks, blocked, precision=lax.Precision.HIGHEST)
        ahead = jnp.einsum('sij,sjk->sik', upper_blocks[:-1], blocked[1:], precision=lax.Precision.HIGHEST)
        behind = jnp.einsum('sji,sjk->sik', upper_blocks[:-1], blocked[:-1], precision=lax.Precision.HIGHEST)
        zero_block = jnp.zeros((1, VAR_DEV, K), jnp.float32)
        product = product + jnp.concatenate([ahead, zero_block], axis=0) + jnp.concatenate([zero_block, behind], axis=0)
        gradient = product.reshape(M, K) - marginal
        moved = effects - step_size * gradient
        effects = jnp.sign(moved) * jnp.maximum(jnp.abs(moved) - threshold[None, :], 0.0)
    effects_low = effects.astype(jnp.bfloat16)
    shrink = 1.0 / math.sqrt(M)
    scores = jnp.dot(dosages, effects_low, preferred_element_type=jnp.float32) * shrink
    stacked = jnp.dot(scores, stack_weights, precision=lax.Precision.HIGHEST, preferred_element_type=jnp.float32)
    return (effects, stacked)
```

```python
import functools
import math

import jax
import jax.numpy as jnp
from jax import lax
from jax.experimental import pallas as pl
from jax.experimental.pallas import tpu as pltpu
from jax.sharding import PartitionSpec as P

ITERS = 3
LANES = 128
MESH = pl.DeviceIdType.MESH

step_size = 0.5


def split(value):
    high = value.astype(jnp.bfloat16)
    low = (value - high.astype(jnp.float32)).astype(jnp.bfloat16)
    return high, low


def rows_of(index, size):
    return pl.ds(pl.multiple_of(index * size, size), size)


def kernel(
    n,
    narrow,
    group,
    shrink,
    start_ref,
    marginal_ref,
    diag_ref,
    upper_ref,
    grid_ref,
    index_ref,
    dosages_ref,
    weights_ref,
    effects_ref,
    stacked_ref,
    diag,
    upper,
    marginal,
    dosages,
    weights,
    index,
    grid,
    diag_high,
    diag_low,
    upper_high,
    upper_low,
    turned_high,
    turned_low,
    effects,
    pair,
    ahead_pair,
    base,
    handed,
    ahead,
    behind,
    threshold,
    strip_scores,
    parts,
    part_sum,
    owned,
    load_sem,
    out_sem,
    ahead_send,
    ahead_recv,
    behind_send,
    behind_recv,
    part_send,
    part_recv,
    owned_send,
    owned_recv,
):
    strip, width = start_ref.shape
    halves = width // LANES
    per_owner = stacked_ref.shape[0]
    groups = n // group
    block = min(256, strip)
    blocks = strip // block
    levels = grid_ref.shape[1]

    me = lax.axis_index("wide") * narrow + lax.axis_index("narrow")
    place = lax.rem(me, group)
    team = me // group
    has_prev = me > 0
    has_next = me < n - 1

    def device(i):
        return (i // narrow, lax.rem(i, narrow))

    prev = device(jnp.maximum(me - 1, 0))
    following = device(jnp.minimum(me + 1, n - 1))

    def mate(distance):
        return team * group + lax.rem(place + distance, group)

    def peer(distance):
        return lax.rem(team + distance, groups) * group + place

    barrier = pltpu.get_barrier_semaphore()

    def greet(where):
        pl.semaphore_signal(barrier, inc=1, device_id=where, device_id_type=MESH)

    greet(device(lax.rem(me + n - 1, n)))
    greet(device(lax.rem(me + 1, n)))
    for distance in range(1, group):
        greet(device(mate(distance)))
    for distance in range(1, groups):
        greet(device(peer(distance)))

    loads = []

    def load(source, target):
        copy = pltpu.make_async_copy(source, target, load_sem.at[len(loads)])
        copy.start()
        loads.append(copy)
        return copy

    def lanes(half):
        return pl.ds(half * LANES, LANES)

    upper_load = load(upper_ref, upper)
    start_loads = [load(start_ref.at[:, lanes(h)], effects.at[0, h]) for h in range(halves)]
    diag_load = load(diag_ref, diag)
    marginal_loads = [load(marginal_ref.at[:, lanes(h)], marginal.at[h]) for h in range(halves)]
    index_load = load(index_ref, index)
    grid_load = load(grid_ref, grid)
    dosages_load = load(dosages_ref, dosages)
    weights_load = load(weights_ref, weights)

    pl.semaphore_wait(barrier, group + groups)

    def effects_copy(sweep, half):
        source = start_ref.at[:, lanes(half)] if sweep == 0 else effects.at[sweep, half]
        return pltpu.make_async_remote_copy(
            src_ref=source,
            dst_ref=ahead.at[sweep, half],
            send_sem=ahead_send.at[sweep, half],
            recv_sem=ahead_recv.at[sweep, half],
            device_id=prev,
            device_id_type=MESH,
        )

    def handed_copy(sweep, half):
        return pltpu.make_async_remote_copy(
            src_ref=handed.at[sweep, half],
            dst_ref=behind.at[sweep, half],
            send_sem=behind_send.at[sweep, half],
            recv_sem=behind_recv.at[sweep, half],
            device_id=following,
            device_id_type=MESH,
        )

    def send_effects(sweep, half):
        @pl.when(has_prev)
        def _():
            effects_copy(sweep, half).start()

    for half in range(halves):
        send_effects(0, half)

    def product(high, low, both, rows):
        wide = jnp.dot(high[rows, :], both[...], preferred_element_type=jnp.float32)
        small = jnp.dot(low[rows, :], both[:, :LANES], preferred_element_type=jnp.float32)
        return wide[:, :LANES] + (wide[:, LANES:] + small)

    def split_effects(value, both, rows):
        high, low = split(value)
        both[rows, :LANES] = high
        both[rows, LANES:] = low

    def each_block(body):
        @pl.loop(0, blocks)
        def _(b):
            body(rows_of(b, block))

    upper_load.wait()

    def turn(rows):
        high, low = split(upper[:, rows].T)
        turned_high[rows, :] = high
        turned_low[rows, :] = low

    for b in range(blocks):
        turn(pl.ds(b * block, block))

    def hand_on(sweep, half):
        @pl.when(has_next)
        def _():
            def body(rows):
                handed[sweep, half, rows, :] = product(turned_high, turned_low, pair.at[half], rows)

            each_block(body)
            handed_copy(sweep, half).start()

    def own_term(sweep, half):
        def body(rows):
            own = product(diag_high, diag_low, pair.at[half], rows)
            gradient = own - marginal[half, rows, :]
            base[half, rows, :] = effects[sweep, half, rows, :] - step_size * gradient

        each_block(body)

    for half in range(halves):
        start_loads[half].wait()

        def body(rows, half=half):
            split_effects(effects[0, half, rows, :], pair.at[half], rows)

        each_block(body)
        hand_on(0, half)

    def split_upper(rows):
        high, low = split(upper[rows, :])
        upper_high[rows, :] = high
        upper_low[rows, :] = low

    each_block(split_upper)
    diag_load.wait()

    def split_diag(rows):
        high, low = split(diag[rows, :])
        diag_high[rows, :] = high
        diag_low[rows, :] = low

    each_block(split_diag)
    for half in range(halves):
        marginal_loads[half].wait()
        own_term(0, half)
    index_load.wait()
    grid_load.wait()
    picked = jnp.zeros((1, width), jnp.float32)
    for level in range(levels):
        picked = jnp.where(index[...] == level, grid[0, level], picked)
    threshold[...] = step_size * picked
    dosages_load.wait()
    weights_load.wait()

    def finish(sweep, half):
        @pl.when(has_next)
        def _():
            effects_copy(sweep, half).wait_recv()

            def body(rows):
                split_effects(ahead[sweep, half, rows, :], ahead_pair, rows)

            each_block(body)

            def add(rows):
                coupled = product(upper_high, upper_low, ahead_pair, rows)
                base[half, rows, :] = base[half, rows, :] - step_size * coupled

            each_block(add)

        @pl.when(has_prev)
        def _():
            handed_copy(sweep, half).wait_recv()

            def add(rows):
                base[half, rows, :] = base[half, rows, :] - step_size * behind[sweep, half, rows, :]

            each_block(add)

        limit = threshold[:, half * LANES : (half + 1) * LANES]

        def shrink_rows(rows):
            moved = base[half, rows, :]
            fresh = moved - jnp.minimum(jnp.maximum(moved, -limit), limit)
            effects[sweep + 1, half, rows, :] = fresh
            split_effects(fresh, pair.at[half], rows)

        each_block(shrink_rows)

    def part_copy(half, distance):
        return pltpu.make_async_remote_copy(
            src_ref=strip_scores.at[half, lax.rem(place + distance, group)],
            dst_ref=parts.at[half, distance],
            send_sem=part_send.at[half, distance],
            recv_sem=part_recv.at[half, distance],
            device_id=device(mate(distance)),
            device_id_type=MESH,
        )

    def owned_copy(half, distance):
        return pltpu.make_async_remote_copy(
            src_ref=part_sum.at[half, lax.rem(team + distance, groups)],
            dst_ref=owned.at[half, distance],
            send_sem=owned_send.at[half, distance],
            recv_sem=owned_recv.at[half, distance],
            device_id=device(peer(distance)),
            device_id_type=MESH,
        )

    out_copies = []

    def score(half):
        copy = pltpu.make_async_copy(
            effects.at[ITERS, half], effects_ref.at[:, lanes(half)], out_sem.at[half]
        )
        copy.start()
        out_copies.append(copy)
        scores = jnp.dot(
            dosages[...], pair[half, :, :LANES], preferred_element_type=jnp.float32
        )
        for t in range(groups):
            for p in range(group):
                at = (t * group + p) * per_owner
                strip_scores[half, p, t * per_owner : (t + 1) * per_owner, :] = scores[
                    at : at + per_owner
                ]
        for distance in range(1, group):
            part_copy(half, distance).start()

    def gather_parts(half):
        total = strip_scores[half, place]
        for distance in range(1, group):
            part_copy(half, distance).wait_recv()
            total = total + parts[half, distance]
        for t in range(groups):
            part_sum[half, t] = total[t * per_owner : (t + 1) * per_owner]
        for distance in range(1, groups):
            owned_copy(half, distance).start()

    def gather_owned(half):
        total = part_sum[half, team]
        for distance in range(1, groups):
            owned_copy(half, distance).wait_recv()
            total = total + owned[half, distance]
        return total * shrink

    for sweep in range(ITERS):
        for half in range(halves):
            finish(sweep, half)
            if sweep + 1 < ITERS:
                send_effects(sweep + 1, half)
                hand_on(sweep + 1, half)
                own_term(sweep + 1, half)
            else:
                score(half)

    for half in range(halves):
        gather_parts(half)
    stacked = None
    for half in range(halves):
        term = jnp.dot(
            gather_owned(half),
            weights[half * LANES : (half + 1) * LANES, :],
            precision=lax.Precision.HIGHEST,
            preferred_element_type=jnp.float32,
        )
        stacked = term if stacked is None else stacked + term
    stacked_ref[...] = stacked

    for copy in out_copies:
        copy.wait()
    for half in range(halves):
        for distance in range(1, group):
            part_copy(half, distance).wait_send()
        for distance in range(1, groups):
            owned_copy(half, distance).wait_send()

    @pl.when(has_prev)
    def _():
        for sweep in range(ITERS):
            for half in range(halves):
                effects_copy(sweep, half).wait_send()

    @pl.when(has_next)
    def _():
        for sweep in range(ITERS):
            for half in range(halves):
                handed_copy(sweep, half).wait_send()


def group_size(n):
    size = 1
    while size * size < n or n % size:
        size += 1
    return size


def solution(mesh):
    wide, narrow = mesh.shape["wide"], mesh.shape["narrow"]
    n = wide * narrow

    def shards(
        effects_start, marginal, ld_diag, ld_upper, penalty_grid, penalty_index, dosages, stack_weights
    ):
        strip, width = effects_start.shape
        halves = width // LANES
        people = dosages.shape[0]
        levels = penalty_grid.shape[0]
        per_owner = people // n
        group = group_size(n)
        groups = n // group
        f32, bf16 = jnp.float32, jnp.bfloat16
        anywhere = pl.BlockSpec(memory_space=pl.ANY)
        dma = pltpu.SemaphoreType.DMA
        call = pl.pallas_call(
            functools.partial(kernel, n, narrow, group, 1.0 / math.sqrt(strip * n)),
            out_shape=(
                jax.ShapeDtypeStruct((strip, width), f32),
                jax.ShapeDtypeStruct((per_owner, width), f32),
            ),
            in_specs=[pl.BlockSpec(memory_space=pltpu.HBM)] * 8,
            out_specs=(anywhere, pl.BlockSpec(memory_space=pltpu.VMEM)),
            scratch_shapes=[
                pltpu.VMEM((strip, strip), f32),
                pltpu.VMEM((strip, strip), f32),
                pltpu.VMEM((halves, strip, LANES), f32),
                pltpu.VMEM((people, strip), bf16),
                pltpu.VMEM((width, width), f32),
                pltpu.VMEM((1, width), jnp.int32),
                pltpu.SMEM((1, levels), f32),
                *[pltpu.VMEM((strip, strip), bf16)] * 6,
                pltpu.VMEM((ITERS + 1, halves, strip, LANES), f32),
                pltpu.VMEM((halves, strip, 2 * LANES), bf16),
                pltpu.VMEM((strip, 2 * LANES), bf16),
                pltpu.VMEM((halves, strip, LANES), f32),
                pltpu.VMEM((ITERS, halves, strip, LANES), f32),
                pltpu.VMEM((ITERS, halves, strip, LANES), f32),
                pltpu.VMEM((ITERS, halves, strip, LANES), f32),
                pltpu.VMEM((1, width), f32),
                pltpu.VMEM((halves, group, groups * per_owner, LANES), f32),
                pltpu.VMEM((halves, group, groups * per_owner, LANES), f32),
                pltpu.VMEM((halves, groups, per_owner, LANES), f32),
                pltpu.VMEM((halves, groups, per_owner, LANES), f32),
                dma((6 + 2 * halves,)),
                dma((halves,)),
                *[dma((ITERS, halves))] * 4,
                *[dma((halves, group))] * 2,
                *[dma((halves, groups))] * 2,
            ],
            compiler_params=pltpu.CompilerParams(
                collective_id=0, has_side_effects=True, vmem_limit_bytes=60 * 2**20
            ),
            cost_estimate=pl.CostEstimate(
                flops=2 * 9 * ITERS * strip * strip * width,
                bytes_accessed=4 * (2 * strip * strip + 3 * strip * width),
                transcendentals=0,
            ),
        )
        return call(
            effects_start,
            marginal,
            ld_diag,
            ld_upper,
            penalty_grid[None, :],
            penalty_index[None, :],
            dosages,
            stack_weights,
        )

    return jax.shard_map(
        shards,
        mesh=mesh,
        in_specs=(
            P(("wide", "narrow"), None),
            P(("wide", "narrow"), None),
            P(("wide", "narrow"), None),
            P(("wide", "narrow"), None),
            P(),
            P(),
            P(None, ("wide", "narrow")),
            P(),
        ),
        out_specs=(P(("wide", "narrow"), None), P(("wide", "narrow"), None)),
        check_vma=False,
    )
```

```python
import functools
import math

import jax
import jax.numpy as jnp
from jax import lax
from jax.experimental import pallas as pl
from jax.experimental.pallas import tpu as pltpu
from jax.sharding import PartitionSpec as P

ITERS = 3
LANES = 128
MESH = pl.DeviceIdType.MESH

step_size = 0.5


def split(value):
    high = value.astype(jnp.bfloat16)
    low = (value - high.astype(jnp.float32)).astype(jnp.bfloat16)
    return high, low


def shrunk(moved, limit):
    return moved - jnp.minimum(jnp.maximum(moved, -limit), limit)


def rows_of(index, size):
    return pl.ds(pl.multiple_of(index * size, size), size)


def kernel(
    n,
    narrow,
    group,
    shrink,
    start_ref,
    marginal_ref,
    diag_ref,
    upper_ref,
    grid_ref,
    index_ref,
    dosages_ref,
    weights_ref,
    moved_ref,
    threshold,
    stacked_ref,
    diag,
    upper,
    marginal,
    dosages,
    weights,
    index,
    grid,
    diag_high,
    diag_low,
    upper_high,
    upper_low,
    turned_high,
    turned_low,
    effects,
    pair,
    ahead_pair,
    base,
    handed,
    ahead,
    behind,
    strip_scores,
    parts,
    part_sum,
    owned,
    load_sem,
    out_sem,
    ahead_send,
    ahead_recv,
    behind_send,
    behind_recv,
    part_send,
    part_recv,
    owned_send,
    owned_recv,
):
    strip, width = start_ref.shape
    halves = width // LANES
    per_owner = stacked_ref.shape[0]
    groups = n // group
    block = row_block(strip)
    blocks = strip // block
    levels = grid_ref.shape[1]

    me = lax.axis_index("wide") * narrow + lax.axis_index("narrow")
    place = lax.rem(me, group)
    team = me // group
    has_prev = me > 0
    has_next = me < n - 1

    def device(i):
        return (i // narrow, lax.rem(i, narrow))

    prev = device(jnp.maximum(me - 1, 0))
    following = device(jnp.minimum(me + 1, n - 1))

    def mate(distance):
        return team * group + lax.rem(place + distance, group)

    def peer(distance):
        return lax.rem(team + distance, groups) * group + place

    barrier = pltpu.get_barrier_semaphore()

    def greet(where):
        pl.semaphore_signal(barrier, inc=1, device_id=where, device_id_type=MESH)

    greet(device(lax.rem(me + n - 1, n)))
    greet(device(lax.rem(me + 1, n)))
    for distance in range(1, group):
        greet(device(mate(distance)))
    for distance in range(1, groups):
        greet(device(peer(distance)))

    loads = []

    def load(source, target):
        copy = pltpu.make_async_copy(source, target, load_sem.at[len(loads)])
        copy.start()
        loads.append(copy)
        return copy

    def lanes(half):
        return pl.ds(half * LANES, LANES)

    upper_load = load(upper_ref, upper)
    start_loads = [load(start_ref.at[:, lanes(h)], effects.at[0, h]) for h in range(halves)]
    diag_load = load(diag_ref, diag)
    marginal_loads = [load(marginal_ref.at[:, lanes(h)], marginal.at[h]) for h in range(halves)]
    index_load = load(index_ref, index)
    grid_load = load(grid_ref, grid)
    dosages_load = load(dosages_ref, dosages)
    weights_load = load(weights_ref, weights)

    pl.semaphore_wait(barrier, group + groups)

    def block_rows(b):
        return pl.ds(b * block, block)

    def effects_copy(sweep, half, b):
        rows = block_rows(b)
        source = start_ref.at[rows, lanes(half)] if sweep == 0 else effects.at[sweep, half, rows]
        return pltpu.make_async_remote_copy(
            src_ref=source,
            dst_ref=ahead.at[sweep, half, rows],
            send_sem=ahead_send.at[sweep, half, b],
            recv_sem=ahead_recv.at[sweep, half, b],
            device_id=prev,
            device_id_type=MESH,
        )

    def handed_copy(sweep, half, b):
        rows = block_rows(b)
        return pltpu.make_async_remote_copy(
            src_ref=handed.at[sweep, half, rows],
            dst_ref=behind.at[sweep, half, rows],
            send_sem=behind_send.at[sweep, half, b],
            recv_sem=behind_recv.at[sweep, half, b],
            device_id=following,
            device_id_type=MESH,
        )

    def send_effects(sweep, half, b):
        @pl.when(has_prev)
        def _():
            effects_copy(sweep, half, b).start()

    for half in range(halves):
        for b in range(blocks):
            send_effects(0, half, b)

    def product(high, low, both, rows):
        wide = jnp.dot(high[rows, :], both[...], preferred_element_type=jnp.float32)
        small = jnp.dot(low[rows, :], both[:, :LANES], preferred_element_type=jnp.float32)
        return wide[:, :LANES] + (wide[:, LANES:] + small)

    def split_effects(value, both, rows):
        high, low = split(value)
        both[rows, :LANES] = high
        both[rows, LANES:] = low

    def each_block(body):
        @pl.loop(0, blocks)
        def _(b):
            body(rows_of(b, block))

    upper_load.wait()

    def turn(rows):
        high, low = split(upper[:, rows].T)
        turned_high[rows, :] = high
        turned_low[rows, :] = low

    for b in range(blocks):
        turn(pl.ds(b * block, block))

    def hand_on(sweep, half):
        @pl.when(has_next)
        def _():
            for b in range(blocks):
                rows = block_rows(b)
                handed[sweep, half, rows, :] = product(turned_high, turned_low, pair.at[half], rows)
                handed_copy(sweep, half, b).start()

    def own_term(sweep, half):
        def body(rows):
            own = product(diag_high, diag_low, pair.at[half], rows)
            gradient = own - marginal[half, rows, :]
            base[half, rows, :] = effects[sweep, half, rows, :] - step_size * gradient

        each_block(body)

    for half in range(halves):
        start_loads[half].wait()

        def body(rows, half=half):
            split_effects(effects[0, half, rows, :], pair.at[half], rows)

        each_block(body)
        hand_on(0, half)

    def split_upper(rows):
        high, low = split(upper[rows, :])
        upper_high[rows, :] = high
        upper_low[rows, :] = low

    each_block(split_upper)
    diag_load.wait()

    def split_diag(rows):
        high, low = split(diag[rows, :])
        diag_high[rows, :] = high
        diag_low[rows, :] = low

    each_block(split_diag)
    for half in range(halves):
        marginal_loads[half].wait()
    index_load.wait()
    grid_load.wait()
    picked = jnp.zeros((1, width), jnp.float32)
    for level in range(levels):
        picked = jnp.where(index[...] == level, grid[0, level], picked)
    threshold[...] = step_size * picked

    @pl.when(me == n - 1)
    def _():
        ahead[...] = jnp.zeros_like(ahead)

    @pl.when(me == 0)
    def _():
        behind[...] = jnp.zeros_like(behind)

    dosages_load.wait()
    weights_load.wait()

    out_copies = []

    def finish(sweep, half):
        last = sweep + 1 == ITERS
        for b in range(blocks):

            @pl.when(has_next)
            def _(b=b):
                effects_copy(sweep, half, b).wait_recv()

            rows = block_rows(b)
            split_effects(ahead[sweep, half, rows, :], ahead_pair, rows)

        limit = threshold[:, half * LANES : (half + 1) * LANES]
        for b in range(blocks):
            rows = block_rows(b)
            coupled = product(upper_high, upper_low, ahead_pair, rows)

            @pl.when(has_prev)
            def _(b=b):
                handed_copy(sweep, half, b).wait_recv()

            moved = base[half, rows, :] - step_size * (coupled + behind[sweep, half, rows, :])
            fresh = shrunk(moved, limit)
            split_effects(fresh, pair.at[half], rows)
            if last:
                base[half, rows, :] = moved
            else:
                effects[sweep + 1, half, rows, :] = fresh
                send_effects(sweep + 1, half, b)
        if last:
            copy = pltpu.make_async_copy(
                base.at[half], moved_ref.at[:, lanes(half)], out_sem.at[half]
            )
            copy.start()
            out_copies.append(copy)

    def part_copy(half, distance):
        return pltpu.make_async_remote_copy(
            src_ref=strip_scores.at[half, lax.rem(place + distance, group)],
            dst_ref=parts.at[half, distance],
            send_sem=part_send.at[half, distance],
            recv_sem=part_recv.at[half, distance],
            device_id=device(mate(distance)),
            device_id_type=MESH,
        )

    def owned_copy(half, distance):
        return pltpu.make_async_remote_copy(
            src_ref=part_sum.at[half, lax.rem(team + distance, groups)],
            dst_ref=owned.at[half, distance],
            send_sem=owned_send.at[half, distance],
            recv_sem=owned_recv.at[half, distance],
            device_id=device(peer(distance)),
            device_id_type=MESH,
        )

    def score(half):
        scores = jnp.dot(
            dosages[...], pair[half, :, :LANES], preferred_element_type=jnp.float32
        )
        for t in range(groups):
            for p in range(group):
                at = (t * group + p) * per_owner
                strip_scores[half, p, t * per_owner : (t + 1) * per_owner, :] = scores[
                    at : at + per_owner
                ]
        for distance in range(1, group):
            part_copy(half, distance).start()

    def gather_parts(half):
        total = strip_scores[half, place]
        for distance in range(1, group):
            part_copy(half, distance).wait_recv()
            total = total + parts[half, distance]
        for t in range(groups):
            part_sum[half, t] = total[t * per_owner : (t + 1) * per_owner]
        for distance in range(1, groups):
            owned_copy(half, distance).start()

    def gather_owned(half):
        total = part_sum[half, team]
        for distance in range(1, groups):
            owned_copy(half, distance).wait_recv()
            total = total + owned[half, distance]
        return total * shrink

    for sweep in range(ITERS):
        for half in range(halves):
            own_term(sweep, half)
            finish(sweep, half)
            if sweep + 1 < ITERS:
                hand_on(sweep + 1, half)
            else:
                score(half)
                if half > 0:
                    gather_parts(half - 1)
    gather_parts(halves - 1)
    stacked = None
    for half in range(halves):
        term = jnp.dot(
            gather_owned(half),
            weights[half * LANES : (half + 1) * LANES, :],
            precision=lax.Precision.HIGHEST,
            preferred_element_type=jnp.float32,
        )
        stacked = term if stacked is None else stacked + term
    stacked_ref[...] = stacked

    for copy in out_copies:
        copy.wait()
    for half in range(halves):
        for distance in range(1, group):
            part_copy(half, distance).wait_send()
        for distance in range(1, groups):
            owned_copy(half, distance).wait_send()

    @pl.when(has_prev)
    def _():
        for sweep in range(ITERS):
            for half in range(halves):
                for b in range(blocks):
                    effects_copy(sweep, half, b).wait_send()

    @pl.when(has_next)
    def _():
        for sweep in range(ITERS):
            for half in range(halves):
                for b in range(blocks):
                    handed_copy(sweep, half, b).wait_send()


def row_block(strip):
    return min(256, strip)


def group_size(n):
    size = 1
    while size * size < n or n % size:
        size += 1
    return size


def solution(mesh):
    wide, narrow = mesh.shape["wide"], mesh.shape["narrow"]
    n = wide * narrow

    def shards(
        effects_start, marginal, ld_diag, ld_upper, penalty_grid, penalty_index, dosages, stack_weights
    ):
        strip, width = effects_start.shape
        halves = width // LANES
        people = dosages.shape[0]
        levels = penalty_grid.shape[0]
        per_owner = people // n
        group = group_size(n)
        groups = n // group
        f32, bf16 = jnp.float32, jnp.bfloat16
        anywhere = pl.BlockSpec(memory_space=pl.ANY)
        dma = pltpu.SemaphoreType.DMA
        call = pl.pallas_call(
            functools.partial(kernel, n, narrow, group, 1.0 / math.sqrt(strip * n)),
            out_shape=(
                jax.ShapeDtypeStruct((strip, width), f32),
                jax.ShapeDtypeStruct((1, width), f32),
                jax.ShapeDtypeStruct((per_owner, width), f32),
            ),
            in_specs=[pl.BlockSpec(memory_space=pltpu.HBM)] * 8,
            out_specs=(anywhere, *[pl.BlockSpec(memory_space=pltpu.VMEM)] * 2),
            scratch_shapes=[
                pltpu.VMEM((strip, strip), f32),
                pltpu.VMEM((strip, strip), f32),
                pltpu.VMEM((halves, strip, LANES), f32),
                pltpu.VMEM((people, strip), bf16),
                pltpu.VMEM((width, width), f32),
                pltpu.VMEM((1, width), jnp.int32),
                pltpu.SMEM((1, levels), f32),
                *[pltpu.VMEM((strip, strip), bf16)] * 6,
                pltpu.VMEM((ITERS, halves, strip, LANES), f32),
                pltpu.VMEM((halves, strip, 2 * LANES), bf16),
                pltpu.VMEM((strip, 2 * LANES), bf16),
                pltpu.VMEM((halves, strip, LANES), f32),
                pltpu.VMEM((ITERS, halves, strip, LANES), f32),
                pltpu.VMEM((ITERS, halves, strip, LANES), f32),
                pltpu.VMEM((ITERS, halves, strip, LANES), f32),
                pltpu.VMEM((halves, group, groups * per_owner, LANES), f32),
                pltpu.VMEM((halves, group, groups * per_owner, LANES), f32),
                pltpu.VMEM((halves, groups, per_owner, LANES), f32),
                pltpu.VMEM((halves, groups, per_owner, LANES), f32),
                dma((6 + 2 * halves,)),
                dma((halves,)),
                *[dma((ITERS, halves, strip // row_block(strip)))] * 4,
                *[dma((halves, group))] * 2,
                *[dma((halves, groups))] * 2,
            ],
            compiler_params=pltpu.CompilerParams(
                collective_id=0, has_side_effects=True, vmem_limit_bytes=60 * 2**20
            ),
            cost_estimate=pl.CostEstimate(
                flops=2 * 9 * ITERS * strip * strip * width,
                bytes_accessed=4 * (2 * strip * strip + 3 * strip * width),
                transcendentals=0,
            ),
        )
        moved, threshold, stacked = call(
            effects_start,
            marginal,
            ld_diag,
            ld_upper,
            penalty_grid[None, :],
            penalty_index[None, :],
            dosages,
            stack_weights,
        )
        return shrunk(moved, threshold), stacked

    return jax.shard_map(
        shards,
        mesh=mesh,
        in_specs=(
            P(("wide", "narrow"), None),
            P(("wide", "narrow"), None),
            P(("wide", "narrow"), None),
            P(("wide", "narrow"), None),
            P(),
            P(),
            P(None, ("wide", "narrow")),
            P(),
        ),
        out_specs=(P(("wide", "narrow"), None), P(("wide", "narrow"), None)),
        check_vma=False,
    )
```

```python
import functools
import math

import jax
import jax.numpy as jnp
from jax import lax
from jax.experimental import pallas as pl
from jax.experimental.pallas import tpu as pltpu
from jax.sharding import PartitionSpec as P

ITERS = 3
LANES = 128
MESH = pl.DeviceIdType.MESH

step_size = 0.5


def split(value):
    high = value.astype(jnp.bfloat16)
    low = (value - high.astype(jnp.float32)).astype(jnp.bfloat16)
    return high, low


def shrunk(moved, limit):
    return moved - jnp.minimum(jnp.maximum(moved, -limit), limit)


def rows_of(index, size):
    return pl.ds(pl.multiple_of(index * size, size), size)


def kernel(
    n,
    narrow,
    group,
    shrink,
    start_ref,
    marginal_ref,
    diag_ref,
    upper_ref,
    grid_ref,
    index_ref,
    dosages_ref,
    weights_ref,
    effects_ref,
    stacked_ref,
    diag,
    upper,
    marginal,
    dosages,
    weights,
    index,
    grid,
    diag_high,
    diag_low,
    upper_high,
    upper_low,
    turned_high,
    turned_low,
    effects,
    pair,
    ahead_pair,
    base,
    handed,
    ahead,
    behind,
    threshold,
    strip_scores,
    parts,
    part_sum,
    owned,
    load_sem,
    out_sem,
    ahead_send,
    ahead_recv,
    behind_send,
    behind_recv,
    part_send,
    part_recv,
    owned_send,
    owned_recv,
):
    strip, width = start_ref.shape
    halves = width // LANES
    per_owner = stacked_ref.shape[0]
    groups = n // group
    block = row_block(strip)
    blocks = strip // block
    levels = grid_ref.shape[1]

    me = lax.axis_index("wide") * narrow + lax.axis_index("narrow")
    place = lax.rem(me, group)
    team = me // group
    has_prev = me > 0
    has_next = me < n - 1

    def device(i):
        return (i // narrow, lax.rem(i, narrow))

    prev = device(jnp.maximum(me - 1, 0))
    following = device(jnp.minimum(me + 1, n - 1))

    def mate(distance):
        return team * group + lax.rem(place + distance, group)

    def peer(distance):
        return lax.rem(team + distance, groups) * group + place

    barrier = pltpu.get_barrier_semaphore()

    def greet(where):
        pl.semaphore_signal(barrier, inc=1, device_id=where, device_id_type=MESH)

    greet(device(lax.rem(me + n - 1, n)))
    greet(device(lax.rem(me + 1, n)))
    for distance in range(1, group):
        greet(device(mate(distance)))
    for distance in range(1, groups):
        greet(device(peer(distance)))

    loads = []

    def load(source, target):
        copy = pltpu.make_async_copy(source, target, load_sem.at[len(loads)])
        copy.start()
        loads.append(copy)
        return copy

    def lanes(half):
        return pl.ds(half * LANES, LANES)

    upper_load = load(upper_ref, upper)
    start_loads = [load(start_ref.at[:, lanes(h)], effects.at[0, h]) for h in range(halves)]
    diag_load = load(diag_ref, diag)
    marginal_loads = [load(marginal_ref.at[:, lanes(h)], marginal.at[h]) for h in range(halves)]
    index_load = load(index_ref, index)
    grid_load = load(grid_ref, grid)
    dosages_load = load(dosages_ref, dosages)
    weights_load = load(weights_ref, weights)

    pl.semaphore_wait(barrier, group + groups)

    def block_rows(b):
        return pl.ds(b * block, block)

    def effects_copy(sweep, half, b):
        rows = block_rows(b)
        source = start_ref.at[rows, lanes(half)] if sweep == 0 else effects.at[sweep, half, rows]
        return pltpu.make_async_remote_copy(
            src_ref=source,
            dst_ref=ahead.at[sweep, half, rows],
            send_sem=ahead_send.at[sweep, half, b],
            recv_sem=ahead_recv.at[sweep, half, b],
            device_id=prev,
            device_id_type=MESH,
        )

    def handed_copy(sweep, half, b):
        rows = block_rows(b)
        return pltpu.make_async_remote_copy(
            src_ref=handed.at[sweep, half, rows],
            dst_ref=behind.at[sweep, half, rows],
            send_sem=behind_send.at[sweep, half, b],
            recv_sem=behind_recv.at[sweep, half, b],
            device_id=following,
            device_id_type=MESH,
        )

    def send_effects(sweep, half, b):
        @pl.when(has_prev)
        def _():
            effects_copy(sweep, half, b).start()

    for b in range(blocks):
        send_effects(0, 0, b)

    def product(high, low, both, rows):
        wide = jnp.dot(high[rows, :], both[...], preferred_element_type=jnp.float32)
        small = jnp.dot(low[rows, :], both[:, :LANES], preferred_element_type=jnp.float32)
        return wide[:, :LANES] + (wide[:, LANES:] + small)

    def split_effects(value, both, rows):
        high, low = split(value)
        both[rows, :LANES] = high
        both[rows, LANES:] = low

    def each_block(body):
        @pl.loop(0, blocks)
        def _(b):
            body(rows_of(b, block))

    upper_load.wait()

    def turn(rows):
        high, low = split(upper[:, rows].T)
        turned_high[rows, :] = high
        turned_low[rows, :] = low

    for b in range(blocks):
        turn(pl.ds(b * block, block))

    def hand_on(sweep, half, sent=True):
        @pl.when(has_next)
        def _():
            for b in range(blocks):
                rows = block_rows(b)
                handed[sweep, half, rows, :] = product(turned_high, turned_low, pair.at[half], rows)
                if sent:
                    handed_copy(sweep, half, b).start()

    def own_term(sweep, half):
        def body(rows):
            own = product(diag_high, diag_low, pair.at[half], rows)
            gradient = own - marginal[half, rows, :]
            base[half, rows, :] = effects[sweep, half, rows, :] - step_size * gradient

        each_block(body)

    for half in range(halves):
        start_loads[half].wait()

        def body(rows, half=half):
            split_effects(effects[0, half, rows, :], pair.at[half], rows)

        each_block(body)
        hand_on(0, half, sent=half == 0)

    def split_upper(rows):
        high, low = split(upper[rows, :])
        upper_high[rows, :] = high
        upper_low[rows, :] = low

    each_block(split_upper)
    diag_load.wait()

    def split_diag(rows):
        high, low = split(diag[rows, :])
        diag_high[rows, :] = high
        diag_low[rows, :] = low

    each_block(split_diag)
    for half in range(halves):
        marginal_loads[half].wait()
    index_load.wait()
    grid_load.wait()
    picked = jnp.zeros((1, width), jnp.float32)
    for level in range(levels):
        picked = jnp.where(index[...] == level, grid[0, level], picked)
    threshold[...] = step_size * picked

    @pl.when(me == n - 1)
    def _():
        ahead[...] = jnp.zeros_like(ahead)

    @pl.when(me == 0)
    def _():
        behind[...] = jnp.zeros_like(behind)

    dosages_load.wait()
    weights_load.wait()

    for half in range(1, halves):

        @pl.when(has_next)
        def _(half=half):
            for b in range(blocks):
                handed_copy(0, half - 1, b).wait_send()
                handed_copy(0, half, b).start()


    out_copies = []

    def finish(sweep, half):
        last = sweep + 1 == ITERS
        for b in range(blocks):

            @pl.when(has_next)
            def _(b=b):
                effects_copy(sweep, half, b).wait_recv()

            rows = block_rows(b)
            split_effects(ahead[sweep, half, rows, :], ahead_pair, rows)

        first = sweep == 0 and half + 1 < halves
        if first:

            @pl.when(has_prev)
            def _():
                for b in range(blocks):
                    handed_copy(sweep, half, b).wait_recv()
                for b in range(blocks):
                    effects_copy(sweep, half, b).wait_send()
                    effects_copy(sweep, half + 1, b).start()

        limit = threshold[:, half * LANES : (half + 1) * LANES]
        for b in range(blocks):
            rows = block_rows(b)
            coupled = product(upper_high, upper_low, ahead_pair, rows)

            if not first:

                @pl.when(has_prev)
                def _(b=b):
                    handed_copy(sweep, half, b).wait_recv()

            moved = base[half, rows, :] - step_size * (coupled + behind[sweep, half, rows, :])
            fresh = shrunk(moved, limit)
            split_effects(fresh, pair.at[half], rows)
            if last:
                base[half, rows, :] = fresh
            else:
                effects[sweep + 1, half, rows, :] = fresh
                send_effects(sweep + 1, half, b)
        if last:
            copy = pltpu.make_async_copy(
                base.at[half], effects_ref.at[:, lanes(half)], out_sem.at[half]
            )
            copy.start()
            out_copies.append(copy)

    def part_copy(half, distance):
        return pltpu.make_async_remote_copy(
            src_ref=strip_scores.at[half, lax.rem(place + distance, group)],
            dst_ref=parts.at[half, distance],
            send_sem=part_send.at[half, distance],
            recv_sem=part_recv.at[half, distance],
            device_id=device(mate(distance)),
            device_id_type=MESH,
        )

    def owned_copy(half, distance):
        return pltpu.make_async_remote_copy(
            src_ref=part_sum.at[half, lax.rem(team + distance, groups)],
            dst_ref=owned.at[half, distance],
            send_sem=owned_send.at[half, distance],
            recv_sem=owned_recv.at[half, distance],
            device_id=device(peer(distance)),
            device_id_type=MESH,
        )

    def score(half):
        scores = jnp.dot(
            dosages[...], pair[half, :, :LANES], preferred_element_type=jnp.float32
        )
        for t in range(groups):
            for p in range(group):
                at = (t * group + p) * per_owner
                strip_scores[half, p, t * per_owner : (t + 1) * per_owner, :] = scores[
                    at : at + per_owner
                ]
        for distance in range(1, group):
            part_copy(half, distance).start()

    def gather_parts(half):
        total = strip_scores[half, place]
        for distance in range(1, group):
            part_copy(half, distance).wait_recv()
            total = total + parts[half, distance]
        for t in range(groups):
            part_sum[half, t] = total[t * per_owner : (t + 1) * per_owner]
        for distance in range(1, groups):
            owned_copy(half, distance).start()

    def gather_owned(half):
        total = part_sum[half, team]
        for distance in range(1, groups):
            owned_copy(half, distance).wait_recv()
            total = total + owned[half, distance]
        return total * shrink

    for sweep in range(ITERS):
        for half in range(halves):
            own_term(sweep, half)
            finish(sweep, half)
            if sweep + 1 < ITERS:
                hand_on(sweep + 1, half)
            else:
                score(half)
                if half > 0:
                    gather_parts(half - 1)
    gather_parts(halves - 1)
    stacked = None
    for half in range(halves):
        term = jnp.dot(
            gather_owned(half),
            weights[half * LANES : (half + 1) * LANES, :],
            precision=lax.Precision.HIGHEST,
            preferred_element_type=jnp.float32,
        )
        stacked = term if stacked is None else stacked + term
    stacked_ref[...] = stacked

    for copy in out_copies:
        copy.wait()
    for half in range(halves):
        for distance in range(1, group):
            part_copy(half, distance).wait_send()
        for distance in range(1, groups):
            owned_copy(half, distance).wait_send()

    @pl.when(has_prev)
    def _():
        for sweep in range(ITERS):
            for half in range(halves):
                if sweep == 0 and half + 1 < halves:
                    continue
                for b in range(blocks):
                    effects_copy(sweep, half, b).wait_send()

    @pl.when(has_next)
    def _():
        for sweep in range(ITERS):
            for half in range(halves):
                if sweep == 0 and half + 1 < halves:
                    continue
                for b in range(blocks):
                    handed_copy(sweep, half, b).wait_send()


def row_block(strip):
    return min(256, strip)


def group_size(n):
    size = 1
    while size * size < n or n % size:
        size += 1
    return size


def solution(mesh):
    wide, narrow = mesh.shape["wide"], mesh.shape["narrow"]
    n = wide * narrow

    def shards(
        effects_start, marginal, ld_diag, ld_upper, penalty_grid, penalty_index, dosages, stack_weights
    ):
        strip, width = effects_start.shape
        halves = width // LANES
        people = dosages.shape[0]
        levels = penalty_grid.shape[0]
        per_owner = people // n
        group = group_size(n)
        groups = n // group
        f32, bf16 = jnp.float32, jnp.bfloat16
        anywhere = pl.BlockSpec(memory_space=pl.ANY)
        dma = pltpu.SemaphoreType.DMA
        call = pl.pallas_call(
            functools.partial(kernel, n, narrow, group, 1.0 / math.sqrt(strip * n)),
            out_shape=(
                jax.ShapeDtypeStruct((strip, width), f32),
                jax.ShapeDtypeStruct((per_owner, width), f32),
            ),
            in_specs=[pl.BlockSpec(memory_space=pltpu.HBM)] * 8,
            out_specs=(anywhere, pl.BlockSpec(memory_space=pltpu.VMEM)),
            scratch_shapes=[
                pltpu.VMEM((strip, strip), f32),
                pltpu.VMEM((strip, strip), f32),
                pltpu.VMEM((halves, strip, LANES), f32),
                pltpu.VMEM((people, strip), bf16),
                pltpu.VMEM((width, width), f32),
                pltpu.VMEM((1, width), jnp.int32),
                pltpu.SMEM((1, levels), f32),
                *[pltpu.VMEM((strip, strip), bf16)] * 6,
                pltpu.VMEM((ITERS, halves, strip, LANES), f32),
                pltpu.VMEM((halves, strip, 2 * LANES), bf16),
                pltpu.VMEM((strip, 2 * LANES), bf16),
                pltpu.VMEM((halves, strip, LANES), f32),
                pltpu.VMEM((ITERS, halves, strip, LANES), f32),
                pltpu.VMEM((ITERS, halves, strip, LANES), f32),
                pltpu.VMEM((ITERS, halves, strip, LANES), f32),
                pltpu.VMEM((1, width), f32),
                pltpu.VMEM((halves, group, groups * per_owner, LANES), f32),
                pltpu.VMEM((halves, group, groups * per_owner, LANES), f32),
                pltpu.VMEM((halves, groups, per_owner, LANES), f32),
                pltpu.VMEM((halves, groups, per_owner, LANES), f32),
                dma((6 + 2 * halves,)),
                dma((halves,)),
                *[dma((ITERS, halves, strip // row_block(strip)))] * 4,
                *[dma((halves, group))] * 2,
                *[dma((halves, groups))] * 2,
            ],
            compiler_params=pltpu.CompilerParams(
                collective_id=0, has_side_effects=True, vmem_limit_bytes=60 * 2**20
            ),
            cost_estimate=pl.CostEstimate(
                flops=2 * 9 * ITERS * strip * strip * width,
                bytes_accessed=4 * (2 * strip * strip + 3 * strip * width),
                transcendentals=0,
            ),
        )
        return call(
            effects_start,
            marginal,
            ld_diag,
            ld_upper,
            penalty_grid[None, :],
            penalty_index[None, :],
            dosages,
            stack_weights,
        )
    return jax.shard_map(
        shards,
        mesh=mesh,
        in_specs=(
            P(("wide", "narrow"), None),
            P(("wide", "narrow"), None),
            P(("wide", "narrow"), None),
            P(("wide", "narrow"), None),
            P(),
            P(),
            P(None, ("wide", "narrow")),
            P(),
        ),
        out_specs=(P(("wide", "narrow"), None), P(("wide", "narrow"), None)),
        check_vma=False,
    )
```

```python
import functools
import math

import jax
import jax.numpy as jnp
from jax import lax
from jax.experimental import pallas as pl
from jax.experimental.pallas import tpu as pltpu
from jax.sharding import PartitionSpec as P

ITERS = 3
LANES = 128
MESH = pl.DeviceIdType.MESH

step_size = 0.5


def split(value):
    high = value.astype(jnp.bfloat16)
    low = (value - high.astype(jnp.float32)).astype(jnp.bfloat16)
    return high, low


def shrunk(moved, limit):
    return moved - jnp.minimum(jnp.maximum(moved, -limit), limit)


def rows_of(index, size):
    return pl.ds(pl.multiple_of(index * size, size), size)


def kernel(
    n,
    narrow,
    group,
    shrink,
    start_ref,
    marginal_ref,
    diag_ref,
    upper_ref,
    grid_ref,
    index_ref,
    dosages_ref,
    weights_ref,
    effects_ref,
    stacked_ref,
    diag,
    upper,
    marginal,
    dosages,
    weights,
    index,
    grid,
    diag_high,
    diag_low,
    upper_high,
    upper_low,
    turned_high,
    turned_low,
    effects,
    pair,
    ahead_pair,
    base,
    handed,
    ahead,
    behind,
    threshold,
    strip_scores,
    parts,
    part_sum,
    owned,
    load_sem,
    out_sem,
    ahead_send,
    ahead_recv,
    behind_send,
    behind_recv,
    part_send,
    part_recv,
    owned_send,
    owned_recv,
):
    strip, width = start_ref.shape
    halves = width // LANES
    per_owner = stacked_ref.shape[0]
    groups = n // group
    block = row_block(strip)
    blocks = strip // block
    levels = grid_ref.shape[1]

    me = lax.axis_index("wide") * narrow + lax.axis_index("narrow")
    place = lax.rem(me, group)
    team = me // group
    has_prev = me > 0
    has_next = me < n - 1

    def device(i):
        return (i // narrow, lax.rem(i, narrow))

    prev = device(jnp.maximum(me - 1, 0))
    following = device(jnp.minimum(me + 1, n - 1))

    def mate(distance):
        return team * group + lax.rem(place + distance, group)

    def peer(distance):
        return lax.rem(team + distance, groups) * group + place

    barrier = pltpu.get_barrier_semaphore()

    def greet(where):
        pl.semaphore_signal(barrier, inc=1, device_id=where, device_id_type=MESH)

    greet(device(lax.rem(me + n - 1, n)))
    greet(device(lax.rem(me + 1, n)))
    for distance in range(1, group):
        greet(device(mate(distance)))
    for distance in range(1, groups):
        greet(device(peer(distance)))

    loads = []

    def load(source, target):
        copy = pltpu.make_async_copy(source, target, load_sem.at[len(loads)])
        copy.start()
        loads.append(copy)
        return copy

    def lanes(half):
        return pl.ds(half * LANES, LANES)

    upper_load = load(upper_ref, upper)
    start_loads = [load(start_ref.at[:, lanes(h)], effects.at[0, h]) for h in range(halves)]
    diag_load = load(diag_ref, diag)
    marginal_loads = [load(marginal_ref.at[:, lanes(h)], marginal.at[h]) for h in range(halves)]
    index_load = load(index_ref, index)
    grid_load = load(grid_ref, grid)
    dosages_load = load(dosages_ref, dosages)
    weights_load = load(weights_ref, weights)

    pl.semaphore_wait(barrier, group + groups)

    def block_rows(b):
        return pl.ds(b * block, block)

    def effects_copy(sweep, half, b):
        rows = block_rows(b)
        source = start_ref.at[rows, lanes(half)] if sweep == 0 else effects.at[sweep, half, rows]
        return pltpu.make_async_remote_copy(
            src_ref=source,
            dst_ref=ahead.at[sweep, half, rows],
            send_sem=ahead_send.at[sweep, half, b],
            recv_sem=ahead_recv.at[sweep, half, b],
            device_id=prev,
            device_id_type=MESH,
        )

    def handed_copy(sweep, half, b):
        rows = block_rows(b)
        return pltpu.make_async_remote_copy(
            src_ref=handed.at[sweep, half, rows],
            dst_ref=behind.at[sweep, half, rows],
            send_sem=behind_send.at[sweep, half, b],
            recv_sem=behind_recv.at[sweep, half, b],
            device_id=following,
            device_id_type=MESH,
        )

    def send_effects(sweep, half, b):
        @pl.when(has_prev)
        def _():
            effects_copy(sweep, half, b).start()

    for b in range(blocks):
        send_effects(0, 0, b)

    def product(high, low, both, rows):
        wide = jnp.dot(high[rows, :], both[...], preferred_element_type=jnp.float32)
        small = jnp.dot(low[rows, :], both[:, :LANES], preferred_element_type=jnp.float32)
        return wide[:, :LANES] + (wide[:, LANES:] + small)

    def split_effects(value, both, rows):
        high, low = split(value)
        both[rows, :LANES] = high
        both[rows, LANES:] = low

    def each_block(body):
        @pl.loop(0, blocks)
        def _(b):
            body(rows_of(b, block))

    upper_load.wait()

    def turn(rows):
        high, low = split(upper[:, rows].T)
        turned_high[rows, :] = high
        turned_low[rows, :] = low

    for b in range(blocks):
        turn(pl.ds(b * block, block))

    def hand_on(sweep, half, sent=True):
        @pl.when(has_next)
        def _():
            for b in range(blocks):
                rows = block_rows(b)
                handed[sweep, half, rows, :] = product(turned_high, turned_low, pair.at[half], rows)
                if sent:
                    handed_copy(sweep, half, b).start()

    def own_term(sweep, half):
        def body(rows):
            own = product(diag_high, diag_low, pair.at[half], rows)
            gradient = own - marginal[half, rows, :]
            base[half, rows, :] = effects[sweep, half, rows, :] - step_size * gradient

        each_block(body)

    for half in range(halves):
        start_loads[half].wait()

        def body(rows, half=half):
            split_effects(effects[0, half, rows, :], pair.at[half], rows)

        each_block(body)
        hand_on(0, half, sent=half == 0)

    def split_upper(rows):
        high, low = split(upper[rows, :])
        upper_high[rows, :] = high
        upper_low[rows, :] = low

    each_block(split_upper)
    diag_load.wait()

    def split_diag(rows):
        high, low = split(diag[rows, :])
        diag_high[rows, :] = high
        diag_low[rows, :] = low

    each_block(split_diag)
    for half in range(halves):
        marginal_loads[half].wait()
    index_load.wait()
    grid_load.wait()
    picked = jnp.zeros((1, width), jnp.float32)
    for level in range(levels):
        picked = jnp.where(index[...] == level, grid[0, level], picked)
    threshold[...] = step_size * picked

    @pl.when(me == n - 1)
    def _():
        ahead[...] = jnp.zeros_like(ahead)

    @pl.when(me == 0)
    def _():
        behind[...] = jnp.zeros_like(behind)

    dosages_load.wait()
    weights_load.wait()

    for half in range(1, halves):

        @pl.when(has_next)
        def _(half=half):
            for b in range(blocks):
                handed_copy(0, half - 1, b).wait_send()
                handed_copy(0, half, b).start()


    out_copies = []

    def finish(sweep, half):
        last = sweep + 1 == ITERS
        for b in range(blocks):

            @pl.when(has_next)
            def _(b=b):
                effects_copy(sweep, half, b).wait_recv()

            rows = block_rows(b)
            split_effects(ahead[sweep, half, rows, :], ahead_pair, rows)

        first = sweep == 0 and half + 1 < halves
        if first:

            @pl.when(has_prev)
            def _():
                for b in range(blocks):
                    handed_copy(sweep, half, b).wait_recv()
                for b in range(blocks):
                    effects_copy(sweep, half, b).wait_send()
                    effects_copy(sweep, half + 1, b).start()

        limit = threshold[:, half * LANES : (half + 1) * LANES]
        for b in range(blocks):
            rows = block_rows(b)
            coupled = product(upper_high, upper_low, ahead_pair, rows)

            if not first:

                @pl.when(has_prev)
                def _(b=b):
                    handed_copy(sweep, half, b).wait_recv()

            moved = base[half, rows, :] - step_size * (coupled + behind[sweep, half, rows, :])
            fresh = shrunk(moved, limit)
            split_effects(fresh, pair.at[half], rows)
            if last:
                base[half, rows, :] = fresh
            else:
                effects[sweep + 1, half, rows, :] = fresh
                send_effects(sweep + 1, half, b)
        if last:
            copy = pltpu.make_async_copy(
                base.at[half], effects_ref.at[:, lanes(half)], out_sem.at[half]
            )
            copy.start()
            out_copies.append(copy)

    def part_copy(half, distance):
        return pltpu.make_async_remote_copy(
            src_ref=strip_scores.at[half, lax.rem(place + distance, group)],
            dst_ref=parts.at[half, distance],
            send_sem=part_send.at[half, distance],
            recv_sem=part_recv.at[half, distance],
            device_id=device(mate(distance)),
            device_id_type=MESH,
        )

    def owned_copy(half, distance):
        return pltpu.make_async_remote_copy(
            src_ref=part_sum.at[half, lax.rem(team + distance, groups)],
            dst_ref=owned.at[half, distance],
            send_sem=owned_send.at[half, distance],
            recv_sem=owned_recv.at[half, distance],
            device_id=device(peer(distance)),
            device_id_type=MESH,
        )

    def score(half):
        scores = jnp.dot(
            dosages[...], pair[half, :, :LANES], preferred_element_type=jnp.float32
        )
        for t in range(groups):
            for p in range(group):
                at = (t * group + p) * per_owner
                strip_scores[half, p, t * per_owner : (t + 1) * per_owner, :] = scores[
                    at : at + per_owner
                ]
        for distance in range(1, group):
            part_copy(half, distance).start()

    def gather_parts(half):
        total = strip_scores[half, place]
        for distance in range(1, group):
            part_copy(half, distance).wait_recv()
            total = total + parts[half, distance]
        for t in range(groups):
            part_sum[half, t] = total[t * per_owner : (t + 1) * per_owner]
        for distance in range(1, groups):
            owned_copy(half, distance).start()

    def gather_owned(half):
        total = part_sum[half, team]
        for distance in range(1, groups):
            owned_copy(half, distance).wait_recv()
            total = total + owned[half, distance]
        return total * shrink

    def stack(half):
        return jnp.dot(
            gather_owned(half),
            weights[half * LANES : (half + 1) * LANES, :],
            precision=lax.Precision.HIGHEST,
            preferred_element_type=jnp.float32,
        )

    for sweep in range(ITERS):
        for half in range(halves):
            own_term(sweep, half)
            if sweep + 1 == ITERS and half > 0:
                gather_parts(half - 1)
            finish(sweep, half)
            if sweep + 1 < ITERS:
                hand_on(sweep + 1, half)
            else:
                score(half)
    stacked = None
    for half in range(halves):
        if half + 1 == halves:
            gather_parts(half)
        term = stack(half)
        stacked = term if stacked is None else stacked + term
    stacked_ref[...] = stacked

    for copy in out_copies:
        copy.wait()
    for half in range(halves):
        for distance in range(1, group):
            part_copy(half, distance).wait_send()
        for distance in range(1, groups):
            owned_copy(half, distance).wait_send()

    @pl.when(has_prev)
    def _():
        for sweep in range(ITERS):
            for half in range(halves):
                if sweep == 0 and half + 1 < halves:
                    continue
                for b in range(blocks):
                    effects_copy(sweep, half, b).wait_send()

    @pl.when(has_next)
    def _():
        for sweep in range(ITERS):
            for half in range(halves):
                if sweep == 0 and half + 1 < halves:
                    continue
                for b in range(blocks):
                    handed_copy(sweep, half, b).wait_send()


def hand_out(effects_ref, stacked_ref, effects_out, stacked_out, sems):
    pieces = sems.shape[0] - 1
    rows = effects_ref.shape[0] // pieces
    copies = [pltpu.make_async_copy(stacked_ref, stacked_out, sems.at[pieces])]
    for p in range(pieces):
        part = pl.ds(p * rows, rows)
        copies.append(
            pltpu.make_async_copy(effects_ref.at[part], effects_out.at[part], sems.at[p])
        )
    for copy in copies:
        copy.start()
    for copy in copies:
        copy.wait()


def row_block(strip):
    return min(256, strip)


def group_size(n):
    size = 1
    while size * size < n or n % size:
        size += 1
    return size


def solution(mesh):
    wide, narrow = mesh.shape["wide"], mesh.shape["narrow"]
    n = wide * narrow

    def shards(
        effects_start, marginal, ld_diag, ld_upper, penalty_grid, penalty_index, dosages, stack_weights
    ):
        strip, width = effects_start.shape
        halves = width // LANES
        people = dosages.shape[0]
        levels = penalty_grid.shape[0]
        per_owner = people // n
        group = group_size(n)
        groups = n // group
        f32, bf16 = jnp.float32, jnp.bfloat16
        anywhere = pl.BlockSpec(memory_space=pl.ANY)
        dma = pltpu.SemaphoreType.DMA
        call = pl.pallas_call(
            functools.partial(kernel, n, narrow, group, 1.0 / math.sqrt(strip * n)),
            out_shape=(
                jax.ShapeDtypeStruct((strip, width), f32),
                jax.ShapeDtypeStruct((per_owner, width), f32),
            ),
            in_specs=[pl.BlockSpec(memory_space=pltpu.HBM)] * 8,
            out_specs=(anywhere, pl.BlockSpec(memory_space=pltpu.VMEM)),
            scratch_shapes=[
                pltpu.VMEM((strip, strip), f32),
                pltpu.VMEM((strip, strip), f32),
                pltpu.VMEM((halves, strip, LANES), f32),
                pltpu.VMEM((people, strip), bf16),
                pltpu.VMEM((width, width), f32),
                pltpu.VMEM((1, width), jnp.int32),
                pltpu.SMEM((1, levels), f32),
                *[pltpu.VMEM((strip, strip), bf16)] * 6,
                pltpu.VMEM((ITERS, halves, strip, LANES), f32),
                pltpu.VMEM((halves, strip, 2 * LANES), bf16),
                pltpu.VMEM((strip, 2 * LANES), bf16),
                pltpu.VMEM((halves, strip, LANES), f32),
                pltpu.VMEM((ITERS, halves, strip, LANES), f32),
                pltpu.VMEM((ITERS, halves, strip, LANES), f32),
                pltpu.VMEM((ITERS, halves, strip, LANES), f32),
                pltpu.VMEM((1, width), f32),
                pltpu.VMEM((halves, group, groups * per_owner, LANES), f32),
                pltpu.VMEM((halves, group, groups * per_owner, LANES), f32),
                pltpu.VMEM((halves, groups, per_owner, LANES), f32),
                pltpu.VMEM((halves, groups, per_owner, LANES), f32),
                dma((6 + 2 * halves,)),
                dma((halves,)),
                *[dma((ITERS, halves, strip // row_block(strip)))] * 4,
                *[dma((halves, group))] * 2,
                *[dma((halves, groups))] * 2,
            ],
            compiler_params=pltpu.CompilerParams(
                collective_id=0, has_side_effects=True, vmem_limit_bytes=60 * 2**20
            ),
            cost_estimate=pl.CostEstimate(
                flops=2 * 9 * ITERS * strip * strip * width,
                bytes_accessed=4 * (2 * strip * strip + 3 * strip * width),
                transcendentals=0,
            ),
        )
        effects, stacked = call(
            effects_start,
            marginal,
            ld_diag,
            ld_upper,
            penalty_grid[None, :],
            penalty_index[None, :],
            dosages,
            stack_weights,
        )
        return pl.pallas_call(
            hand_out,
            out_shape=(
                jax.ShapeDtypeStruct(effects.shape, f32),
                jax.ShapeDtypeStruct(stacked.shape, f32),
            ),
            in_specs=[anywhere] * 2,
            out_specs=(anywhere, anywhere),
            scratch_shapes=[dma((math.gcd(strip // 8, 8) + 1,))],
            compiler_params=pltpu.CompilerParams(vmem_limit_bytes=60 * 2**20),
        )(effects, stacked)

    return jax.shard_map(
        shards,
        mesh=mesh,
        in_specs=(
            P(("wide", "narrow"), None),
            P(("wide", "narrow"), None),
            P(("wide", "narrow"), None),
            P(("wide", "narrow"), None),
            P(),
            P(),
            P(None, ("wide", "narrow")),
            P(),
        ),
        out_specs=(P(("wide", "narrow"), None), P(("wide", "narrow"), None)),
        check_vma=False,
    )
```
